256 devices in a mesh: row: 32 (over z, y), col: 8 (over x, core).
Axes of the slice: x: 4, y: 4, z: 8, core: 2. Of those that a mesh axis runs over, the one named last changes fastest.
Arguments:
- vectors: bfloat16 [131072, 256], P(('row', 'col'))
- tile_values: bfloat16 [32, 8, 80, 256, 256], P('row', 'col')
- tile_row: int32 [32, 8, 80], P('row', 'col'), may hold values from 0 to 15, as said below
- tile_col: int32 [32, 8, 80], P('row', 'col'), may hold values from 0 to 63, as said below
- counts: int32 [32, 8], P('row', 'col'), may hold values from 40 to 80, as said below
Outputs:
- basis: float32 [131072, 256], P(('row', 'col'))
- factor: float32 [256, 256], replicated
The draws below stay inside these ranges and needn't reach their ends.
Inputs may be any that keep to these rules, and one draw needn't show every extreme that they name: Within one device the pairs (tile_row, tile_col) of its slots are distinct, and every tile row of a block row has a slot on every device below counts. `tile_col`: column index of a slot's tile within the device's column set. `counts`: some device fills all 80 slots in every draw.
All inputs are finite; a program needn't handle non-finite values.
Results may differ from the reference program's by a relative error of at most 0.0003.
Values may be sent and summed in bfloat16 or wider, within the bound.
No kernel may reach another device: no remote copies, remote signals or barrier semaphores. Data moves between devices by JAX's collectives and lax.ppermute only.
A program may use at most 128 MiB of HBM per device.

```python
import math
import jax
import jax.numpy as jnp
from jax import lax

K = 256
TB = 256
S = 512
TILES = 80
TROWS = 16
TCOLS = 64
NROWS = 131072
N_ROW = 32
N_COL = 8


def tile_pattern(key):
    devices_all = N_ROW * N_COL
    base = jax.random.fold_in(key, 4242)
    row_keys = jax.random.split(jax.random.fold_in(base, 1), devices_all)
    row_perms = jax.vmap(lambda single: jax.random.permutation(single, TROWS))(row_keys)
    col_keys = jax.random.split(jax.random.fold_in(base, 2), devices_all * TROWS)
    col_perms = jax.vmap(lambda single: jax.random.permutation(single, TCOLS))(col_keys)
    col_perms = col_perms.reshape(devices_all, TROWS, TCOLS)
    slots = jnp.arange(TILES, dtype=jnp.int32)
    member = slots % TROWS
    layer = slots // TROWS
    rows_out = row_perms[:, member]
    cols_out = col_perms[:, member, layer]
    return (rows_out.reshape(N_ROW, N_COL, TILES).astype(jnp.int32), cols_out.reshape(N_ROW, N_COL, TILES).astype(jnp.int32))


def draw_tile_row(key, part):
    return tile_pattern(key)[0]


def draw_tile_col(key, part):
    return tile_pattern(key)[1]


def draw_counts(key, part):
    devices_all = N_ROW * N_COL
    first, second, third = jax.random.split(key, 3)
    values = jax.random.randint(first, (devices_all,), TILES // 2, TILES + 1)
    fullest = jax.random.randint(second, (), 0, devices_all)
    emptiest = (fullest + 1 + jax.random.randint(third, (), 0, devices_all - 1)) % devices_all
    index = jnp.arange(devices_all)
    values = jnp.where(index == fullest, TILES, values)
    values = jnp.where(index == emptiest, TILES // 2, values)
    return values.reshape(N_ROW, N_COL).astype(jnp.int32)


def draw_vectors(key, part):
    first = jax.random.fold_in(key, 17)
    values = jax.random.normal(first, (NROWS, K), jnp.float32)
    return values.astype(jnp.bfloat16)


def draw_tile_values(key, part):
    first, second = jax.random.split(key)
    shape = (N_ROW, N_COL, TILES, TB, TB)
    trend = jnp.sqrt(1.0 + 2.0 * jnp.arange(N_ROW, dtype=jnp.float32) / (N_ROW - 1))
    values = jax.random.normal(first, shape, jnp.float32)
    row_scale = jnp.exp(jax.random.uniform(second, (N_ROW, N_COL, TILES, TB, 1), jnp.float32, math.log(0.3), math.log(3.0)))
    values = values * row_scale * trend[:, None, None, None, None] / math.sqrt(4.0 * TB)
    return values.astype(jnp.bfloat16)


def setup_inputs(seed: int = 0) -> dict:
    splits = jax.random.split(jax.random.key(seed), 6)
    vectors = draw_vectors(jax.random.fold_in(splits[5], 71), 0)
    tile_values = draw_tile_values(jax.random.fold_in(splits[5], 71), 0)
    tile_row = draw_tile_row(jax.random.fold_in(splits[5], 71), 0)
    tile_col = draw_tile_col(jax.random.fold_in(splits[5], 71), 0)
    counts = draw_counts(jax.random.fold_in(splits[5], 71), 0)
    return {"vectors": vectors, "tile_values": tile_values, "tile_row": tile_row, "tile_col": tile_col, "counts": counts}


def reference(vectors, tile_values, tile_row, tile_col, counts):
    grid = vectors.reshape(N_ROW, N_COL, S, K)
    slots = jnp.arange(TILES, dtype=jnp.int32)

    def block_row(rindex):

        def one_column(cindex):
            column_set = lax.dynamic_index_in_dim(grid, cindex, axis=1, keepdims=False)
            column_set = column_set.reshape(TCOLS, TB, K)
            picked = column_set[tile_col[rindex, cindex]]
            tiles = tile_values[rindex, cindex].astype(jnp.float32)
            prods = jnp.einsum('tij,tjk->tik', tiles, picked.astype(jnp.float32))
            valid = (slots < counts[rindex, cindex]).astype(jnp.float32)
            prods = prods * valid[:, None, None]
            return jax.ops.segment_sum(prods, tile_row[rindex, cindex], num_segments=TROWS)
        parts = lax.map(one_column, jnp.arange(N_COL, dtype=jnp.int32))
        return jnp.sum(parts, axis=0)
    panel = lax.map(block_row, jnp.arange(N_ROW, dtype=jnp.int32)).reshape(NROWS, K)
    gram = jnp.dot(panel.T, panel, precision=lax.Precision.HIGHEST) / NROWS
    lower = jnp.linalg.cholesky(gram)
    basis = jax.scipy.linalg.solve_triangular(lower, panel.T, lower=True).T
    return (basis, lower.T)
```

```python
import functools

import jax
import jax.numpy as jnp
from jax import lax
from jax.experimental import pallas as pl
from jax.experimental.pallas import tpu as pltpu
from jax.sharding import PartitionSpec as P

HIGH = lax.Precision.HIGHEST
NZ, NY, NX = 8, 4, 4
EARLY = 208
BATCH = 4


def from_y(a, d):
    return lax.ppermute(a, "row", [(z * NY + y, z * NY + (y - d) % NY) for z in range(NZ) for y in range(NY)])


def from_z(a, d):
    return lax.ppermute(a, "row", [(z * NY + y, (z - d) % NZ * NY + y) for z in range(NZ) for y in range(NY)])


def from_x(a, d):
    return lax.ppermute(a, "col", [(x * 2 + c, (x - d) % NX * 2 + c) for x in range(NX) for c in range(2)])


def xor_y(a, k):
    return lax.ppermute(a, "row", [(i, i ^ k) for i in range(NZ * NY)])


def xor_z(a, k):
    return lax.ppermute(a, "row", [(i, i ^ (k * NY)) for i in range(NZ * NY)])


def xor_x(a, k):
    return lax.ppermute(a, "col", [(i, i ^ (2 * k)) for i in range(2 * NX)])


def other_core(a):
    return lax.ppermute(a, "col", [(i, i ^ 1) for i in range(2 * NX)])


def gathered(v):
    a, b = v[:EARLY], v[EARLY:]
    ay = jnp.stack([a, from_y(a, 1), from_y(a, 2), from_y(a, 3)])
    up, down = [ay], [ay]
    bup, bdown = [b], [b]
    for _ in range(3):
        bup.append(from_z(bup[-1], 1))
        bdown.append(from_z(bdown[-1], -1))
    half = (v.shape[0] - EARLY) // 32 * 16
    far = [from_z(bup[3][:half], 1), from_z(bdown[3][half:], -1)]
    bz = jnp.stack(bup + [jnp.concatenate(far)] + bdown[:0:-1])
    for _ in range(3):
        up.append(from_z(up[-1], 1))
        down.append(from_z(down[-1], -1))
    pieces = [(i % NZ, 1, (0, 0, NY), ay) for i in range(1)]
    for i in range(1, 4):
        pieces += [(i, 1, (0, 0, NY), up[i]), (NZ - i, 1, (0, 0, NY), down[i])]
    pieces += [
        (4, 1, (0, 0, 2), from_z(up[3][:2], 1)),
        (4, 1, (0, 2, 2), from_z(down[3][2:], -1)),
    ]
    b1, b3 = from_y(bz, 1), from_y(bz, -1)
    pieces += [(0, 0, (0, 0, NZ), bz), (1, 0, (0, 0, NZ), b1), (3, 0, (0, 0, NZ), b3)]
    pieces += [
        (2, 0, (0, 0, NZ // 2), from_y(b1[: NZ // 2], 1)),
        (2, 0, (0, NZ // 2, NZ // 2), from_y(b3[NZ // 2 :], -1)),
    ]
    return [p[:3] for p in pieces], [p[3] for p in pieces]


def product_kernel(places, slots, me, rows, cols, count, tiles, *refs):
    n = len(places)
    pieces, out = refs[:n], refs[n]
    held, graph, piece_sems, tile_sems = refs[n + 1 :]
    mz, my, mx, mc = me[0], me[1], me[2], me[3]
    filled = count[0]
    copies = []
    for i, ((at, early, (_, lo, size)), piece) in enumerate(zip(places, pieces, strict=True)):
        if early:
            to = held.at[at, pl.ds(lo, size), pl.ds(0, EARLY)]
        else:
            to = held.at[pl.ds(lo, size), at, pl.ds(EARLY, held.shape[2] - EARLY)]
        copies.append(pltpu.make_async_copy(piece, to, piece_sems.at[i]))
    tile_copies = [
        pltpu.make_async_copy(tiles.at[pl.ds(i, BATCH)], graph.at[pl.ds(i, BATCH)], tile_sems.at[i // BATCH])
        for i in range(0, slots, BATCH)
    ]
    for c in copies + tile_copies:
        c.start()
    out[...] = jnp.zeros_like(out)
    for c in copies + tile_copies:
        c.wait()

    def batch(b, carry):
        for i in range(BATCH):
            s = b * BATCH + i
            q = cols[s] // 2
            part = cols[s] % 2
            dz = lax.rem(q // NY - mz + NZ, NZ)
            dy = lax.rem(q % NY - my + NY, NY)
            r = rows[s]
            c = r // 2
            dx = lax.rem(c // 2 - mx + NX, NX)
            place = jnp.where(c % 2 == mc, 0, 2 * NX) + dx * 2 + r % 2
            place = jnp.where(s < filled, place, 4 * NX)
            v = held[dz, dy, pl.ds(pl.multiple_of(part * 256, 256), 256), :]
            out[place] += jnp.dot(graph[s], v, preferred_element_type=jnp.float32)
        return carry

    lax.fori_loop(0, (filled + BATCH - 1) // BATCH, batch, 0)


def products(me, rows, cols, count, tiles, places, pieces, width):
    slots = tiles.shape[0]
    smem = pl.BlockSpec(memory_space=pltpu.SMEM)
    hbm = pl.BlockSpec(memory_space=pl.ANY)
    return pl.pallas_call(
        functools.partial(product_kernel, places, slots),
        out_shape=jax.ShapeDtypeStruct((4 * NX + 1, 256, width), jnp.float32),
        in_specs=[smem] * 4 + [hbm] * (1 + len(pieces)),
        out_specs=pl.BlockSpec(memory_space=pltpu.VMEM),
        scratch_shapes=[
            pltpu.VMEM((NZ, NY, 512, width), jnp.bfloat16),
            pltpu.VMEM(tiles.shape, jnp.bfloat16),
            pltpu.SemaphoreType.DMA((len(pieces),)),
            pltpu.SemaphoreType.DMA((slots // BATCH,)),
        ],
        compiler_params=pltpu.CompilerParams(vmem_limit_bytes=40 * 2**20),
    )(me, rows, cols, count, tiles, *pieces)


def dot_tn(a, b):
    return lax.dot_general(a, b, (((0,), (0,)), ((), ())), precision=HIGH, preferred_element_type=jnp.float32)


def dot_nt(a, b):
    return lax.dot_general(a, b, (((1,), (1,)), ((), ())), precision=HIGH, preferred_element_type=jnp.float32)


def dot_nn(a, b):
    return jnp.dot(a, b, precision=HIGH, preferred_element_type=jnp.float32)


def gram_kernel(total, me, p0, p1, p2, p3, panel, gram):
    p = (p0[...] + p1[...]) + (p2[...] + p3[...])
    panel[...] = p
    g = dot_tn(p, p) / total
    mx, mc = me[2], me[3]
    step = g.shape[0] // (2 * NX)
    for c in range(2):
        for x in range(NX):
            i = c * NX + x
            gram[c ^ mc, x ^ mx] = g[i * step : (i + 1) * step]


def factored(a, n):
    blocks = n // 8
    sub = lax.broadcasted_iota(jnp.int32, (8, n), 0)
    lane = lax.broadcasted_iota(jnp.int32, (8, n), 1)
    rows = [a[8 * i : 8 * i + 8] for i in range(blocks)]
    inv = [jnp.where(lane == sub + 8 * i, 1.0, 0.0).astype(jnp.float32) for i in range(blocks)]
    upper = []
    lower_inv = []

    def spread(x, k):
        return jnp.broadcast_to(x[k : k + 1, :], (8, n))

    for b in range(blocks):
        col = [
            {i: jnp.broadcast_to(rows[i][:, 8 * b + k : 8 * b + k + 1], (8, n)) for i in range(b, blocks)}
            for k in range(8)
        ]
        mult = []
        pivots = jnp.ones((8, n), jnp.float32)
        for k in range(8):
            d = spread(col[k][b], k)
            pivots = jnp.where(sub == k, d, pivots)
            rec = 1.0 / d
            m = {i: col[k][i] * rec for i in range(b, blocks)}
            m[b] = jnp.where(sub > k, m[b], 0.0)
            for j in range(k + 1, 8):
                u = spread(col[j][b], k)
                for i in range(b, blocks):
                    col[j][i] = col[j][i] - m[i] * u
            mult.append(m)
            rows[b] = rows[b] - m[b] * spread(rows[b], k)
            inv[b] = inv[b] - m[b] * spread(inv[b], k)
        for k in range(8):
            r, w = spread(rows[b], k), spread(inv[b], k)
            for i in range(b + 1, blocks):
                rows[i] = rows[i] - mult[k][i] * r
                inv[i] = inv[i] - mult[k][i] * w
        scale = lax.rsqrt(pivots)
        upper.append(jnp.where(lane >= sub + 8 * b, rows[b] * scale, 0.0))
        lower_inv.append(inv[b] * scale)
    return jnp.concatenate(upper), jnp.concatenate(lower_inv)


def finish_kernel(me, mine, theirs, panel, basis, factor, gram):
    mx, mc = me[2], me[3]
    step = gram.shape[0] // (2 * NX)
    for k in range(NX):
        own = mc * NX + (mx ^ k)
        far = (1 - mc) * NX + (mx ^ k)
        gram[pl.ds(pl.multiple_of(own * step, step), step)] = mine[k]
        gram[pl.ds(pl.multiple_of(far * step, step), step)] = theirs[k]
    h = gram.shape[0] // 2
    u1, w1 = factored(gram[:h, :h], h)
    l21 = dot_nt(gram[h:, :h], w1)
    u2, w2 = factored(gram[h:, h:] - dot_nt(l21, l21), h)
    q1 = dot_nt(panel[:, :h], w1)
    basis[:, :h] = q1
    basis[:, h:] = dot_nt(panel[:, h:] - dot_nt(q1, l21), w2)
    factor[:h, :h] = u1
    factor[:h, h:] = l21.T
    factor[h:, :h] = jnp.zeros((h, h), jnp.float32)
    factor[h:, h:] = u2


def on_device(vectors, tile_values, tile_row, tile_col, counts):
    slab, width = vectors.shape
    total = slab * lax.axis_size("row") * lax.axis_size("col")
    row, col = lax.axis_index("row"), lax.axis_index("col")
    me = jnp.stack([row // NY, row % NY, col // 2, col % 2]).astype(jnp.int32)
    smem = pl.BlockSpec(memory_space=pltpu.SMEM)
    vmem = pl.BlockSpec(memory_space=pltpu.VMEM)
    params = pltpu.CompilerParams(vmem_limit_bytes=24 * 2**20)

    places, pieces = gathered(vectors)
    parts = products(
        me, tile_row[0, 0], tile_col[0, 0], counts[0], tile_values[0, 0], places, pieces, width
    )
    away = other_core(parts[2 * NX : 4 * NX])
    pair = (parts[: 2 * NX] + away).reshape(NX, slab, width)
    arrived = [from_x(pair[d], -d) for d in (1, 2, 3)]
    panel, gram = pl.pallas_call(
        functools.partial(gram_kernel, total),
        out_shape=(
            jax.ShapeDtypeStruct((slab, width), jnp.float32),
            jax.ShapeDtypeStruct((2, NX, width // (2 * NX), width), jnp.float32),
        ),
        in_specs=[smem] + [vmem] * 4,
        out_specs=(vmem, vmem),
        compiler_params=params,
    )(me, pair[0], *arrived)
    gram = gram[0] + other_core(gram[1])
    gram = (gram[0] + xor_x(gram[1], 1)) + (xor_x(gram[2], 2) + xor_x(gram[3], 3))
    gram = (gram + xor_y(gram, 1)) + (xor_y(gram, 2) + xor_y(gram, 3))
    z = [gram] + [xor_z(gram, k) for k in range(1, NZ)]
    gram = ((z[0] + z[1]) + (z[2] + z[3])) + ((z[4] + z[5]) + (z[6] + z[7]))
    mine = jnp.stack([gram] + [xor_x(gram, k) for k in range(1, NX)])
    theirs = other_core(mine)
    basis, factor = pl.pallas_call(
        finish_kernel,
        out_shape=(
            jax.ShapeDtypeStruct((slab, width), jnp.float32),
            jax.ShapeDtypeStruct((width, width), jnp.float32),
        ),
        in_specs=[smem] + [vmem] * 3,
        out_specs=(vmem, vmem),
        scratch_shapes=[pltpu.VMEM((width, width), jnp.float32)],
        compiler_params=params,
    )(me, mine, theirs, panel)
    return basis, factor


def solution(mesh):
    return jax.shard_map(
        on_device,
        mesh=mesh,
        in_specs=(
            P(("row", "col"), None),
            P("row", "col", None, None, None),
            P("row", "col", None),
            P("row", "col", None),
            P("row", "col"),
        ),
        out_specs=(P(("row", "col"), None), P()),
        check_vma=False,
    )
```

```python
import functools

import jax
import jax.numpy as jnp
from jax import lax
from jax.experimental import pallas as pl
from jax.experimental.pallas import tpu as pltpu
from jax.sharding import PartitionSpec as P

HIGH = lax.Precision.HIGHEST
NZ, NY, NX = 8, 4, 4
EARLY = 192
BATCH = 4
VMEM_LIMIT = 54 * 2**20


def from_y(a, d):
    return lax.ppermute(a, "row", [(z * NY + y, z * NY + (y - d) % NY) for z in range(NZ) for y in range(NY)])


def from_z(a, d):
    return lax.ppermute(a, "row", [(z * NY + y, (z - d) % NZ * NY + y) for z in range(NZ) for y in range(NY)])


def from_x(a, d):
    return lax.ppermute(a, "col", [(x * 2 + c, (x - d) % NX * 2 + c) for x in range(NX) for c in range(2)])


def xor_y(a, k):
    return lax.ppermute(a, "row", [(i, i ^ k) for i in range(NZ * NY)])


def xor_z(a, k):
    return lax.ppermute(a, "row", [(i, i ^ (k * NY)) for i in range(NZ * NY)])


def xor_x(a, k):
    return lax.ppermute(a, "col", [(i, i ^ (2 * k)) for i in range(2 * NX)])


def other_core(a):
    return lax.ppermute(a, "col", [(i, i ^ 1) for i in range(2 * NX)])


def stages(v):
    a, b = v[:EARLY], v[EARLY:]
    n = b.shape[0]
    h, w = n // 2, NY * EARLY
    together = lax.optimization_barrier
    join = jnp.concatenate

    def early(dz, dys=range(NY)):
        return [(i * EARLY, EARLY, dz, dy, 0) for i, dy in enumerate(dys)]

    def late(at, dz, dy):
        if dz < 5:
            return [(at, n, dz, dy, EARLY)]
        return [(at, h, dz, dy, EARLY + h), (at + h, h, dz, dy, EARLY)]

    def across(at, dzs, second):
        return [(at + i * h, h, dz, 2, EARLY + h * (second != (dz > 4))) for i, dz in enumerate(dzs)]

    def halves(x, count, second):
        return [x[i * n + h * second : i * n + h * second + h] for i in range(count)]

    ay1, ay3, bz1, bz7, ay2 = together(
        (from_y(a, 1), from_y(a, -1), from_z(b, 1), from_z(join([b[h:], b[:h]]), -1), from_y(a, 2))
    )
    up1, down1 = join([a, ay1, ay2, ay3, bz1]), join([a, ay1, ay2, ay3, bz7])
    b0 = join([b, bz1, bz7])
    up2, down2, y1, y3 = together((from_z(up1, 1), from_z(down1, -1), from_y(b0, 1), from_y(b0, -1)))
    near = [(up1, early(0)), (up2, early(1)), (down2, early(7))]
    for x, dy in ((b0, 0), (y1, 1), (y3, 3)):
        near.append((x, [p for i, dz in enumerate((0, 1, 7)) for p in late(i * n, dz, dy)]))
    b1 = [up2[w:], down2[w:]]
    up3, down3, z1, z3 = together(
        (
            from_z(up2, 1),
            from_z(down2, -1),
            from_y(join(b1 + halves(y1, 3, 0)), 1),
            from_y(join(b1 + halves(y3, 3, 1)), -1),
        )
    )
    near += [(up3, early(2)), (down3, early(6)), (up2, late(w, 2, 0)), (down2, late(w, 6, 0))]
    near += [
        (z1, late(0, 2, 1) + late(n, 6, 1) + across(2 * n, (0, 1, 7), 0)),
        (z3, late(0, 2, 3) + late(n, 6, 3) + across(2 * n, (0, 1, 7), 1)),
    ]
    b2 = [up3[w:], down3[w:]]
    up4, down4, y1, y3 = together(
        (
            from_z(up3[: w + h], 1),
            from_z(down3[: w + h], -1),
            from_y(join(b2 + halves(z1, 2, 0)), 1),
            from_y(join(b2 + halves(z3, 2, 1)), -1),
        )
    )
    near += [(up3, late(w, 3, 0)), (down3, late(w, 5, 0))]
    near += [(up4, early(3)), (down4, early(5))]
    near += [
        (y1, late(0, 3, 1) + late(n, 5, 1) + across(2 * n, (2, 6), 0)),
        (y3, late(0, 3, 3) + late(n, 5, 3) + across(2 * n, (2, 6), 1)),
    ]
    b4 = join([up4[w:], down4[w:]])
    up5, down5, z1, z3, z2 = together(
        (
            from_z(up4[: w // 2], 1),
            from_z(down4[w // 2 : w], -1),
            from_y(join([b4] + halves(y1, 2, 0)), 1),
            from_y(join([b4] + halves(y3, 2, 1)), -1),
            from_y(b4, 2),
        )
    )
    far = [
        (up5, early(4, (0, 1))),
        (down5, early(4, (2, 3))),
        (b4, late(0, 4, 0)),
        (z1, late(0, 4, 1) + across(n, (3, 5), 0)),
        (z2, late(0, 4, 2)),
        (z3, late(0, 4, 3) + across(n, (3, 5), 1)),
        (up4, [early(3)[2]]),
        (down4, [early(5)[2]]),
    ]
    return near, far


def merged(pieces):
    arrays = []
    for x, parts in pieces:
        for known, has in arrays:
            if known is x:
                has.extend(parts)
                break
        else:
            arrays.append((x, list(parts)))
    return arrays


def multiply(shard, place, listed, filled, tiles, places, pieces, out, held, graph, sems, tile_sems, where, start=None):
    copies = []
    for parts, piece in zip(places, pieces, strict=True):
        for at, size, dz, dy, first in parts:
            to = held.at[where(dz, dy), pl.ds(first, size)]
            copies.append(pltpu.make_async_copy(piece.at[pl.ds(at, size)], to, sems.at[len(copies)]))
    for c in copies:
        c.start()
    batches = (filled + BATCH - 1) // BATCH

    def fetch(b, carry):
        for i in range(BATCH):
            k = b * BATCH + i
            pltpu.make_async_copy(tiles.at[listed[k]], graph.at[k], tile_sems.at[b]).start()
        return carry

    lax.fori_loop(0, batches, fetch, 0)
    for c in copies:
        c.wait()
    if start is not None:
        start.wait()

    def batch(b, carry):
        pltpu.make_async_copy(
            tiles.at[pl.ds(0, BATCH)], graph.at[pl.ds(b * BATCH, BATCH)], tile_sems.at[b]
        ).wait()
        for i in range(BATCH):
            k = b * BATCH + i
            at = jnp.where(k < filled, place[k], 4 * NX)
            part = shard[k]
            v = held[lax.shift_right_logical(part, 1), pl.ds(pl.multiple_of((part & 1) * 256, 256), 256), :]
            out[at] += jnp.dot(graph[k], v, preferred_element_type=jnp.float32)
        return carry

    lax.fori_loop(0, batches, batch, 0)


def near_kernel(places, me, rows, cols, count, tiles, *refs):
    n = len(places)
    pieces, out = refs[:n], refs[n]
    far_list, far_shard, far_place, far_count = refs[n + 1 : n + 5]
    held, graph, listed, shard, place, sems, tile_sems = refs[n + 5 :]
    mz, my, mx, mc = me[0], me[1], me[2], me[3]

    def where(dz, dy):
        return dz * NY + dy

    def pad(lists, at):
        for i in range(BATCH):
            for x in lists:
                x[at + i] = 0

    def sort(s, counts):
        near, far = counts
        part = cols[s]
        dz = (lax.shift_right_logical(part, 3) - mz) & (NZ - 1)
        dy = (lax.shift_right_logical(part, 1) - my) & (NY - 1)
        r = rows[s]
        c = lax.shift_right_logical(r, 1)
        dx = (lax.shift_right_logical(c, 1) - mx) & (NX - 1)
        to = ((c & 1) ^ mc) * (2 * NX) + dx * 2 + (r & 1)
        distant = (dz == 4) | ((dy == 2) & ((dz == 3) | (dz == 5)))

        @pl.when(distant)
        def _():
            far_list[far] = s
            far_shard[far] = jnp.where(dz == 4, dy, jnp.where(dz == 5, 5, 4)) * 2 + (part & 1)
            far_place[far] = to

        @pl.when(jnp.logical_not(distant))
        def _():
            listed[near] = s
            shard[near] = (dz * NY + dy) * 2 + (part & 1)
            place[near] = to

        step = distant.astype(jnp.int32)
        return near + 1 - step, far + step

    near, far = lax.fori_loop(0, count[0], sort, (0, 0))
    pad((listed, shard, place), near)
    pad((far_list, far_shard, far_place), far)
    far_count[0] = far
    out[...] = jnp.zeros_like(out)
    multiply(shard, place, listed, near, tiles, places, pieces, out, held, graph, sems, tile_sems, where)


def far_kernel(places, listed, shard, place, count, tiles, before, *refs):
    n = len(places)
    pieces, kept, sent = refs[:n], refs[n], refs[n + 1]
    held, graph, total, sum_sems, sems, tile_sems = refs[n + 2 :]
    half = 2 * NX

    def where(dz, dy):
        return dy if dz == 4 else 4 + (dz == 5)

    start = pltpu.make_async_copy(before.at[pl.ds(0, 2 * half)], total.at[pl.ds(0, 2 * half)], sum_sems.at[0])
    start.start()
    multiply(
        shard, place, listed, count[0], tiles, places, pieces, total, held, graph, sems, tile_sems, where, start
    )
    ends = [
        pltpu.make_async_copy(total.at[pl.ds(half, half)], sent, sum_sems.at[0]),
        pltpu.make_async_copy(total.at[pl.ds(0, half)], kept, sum_sems.at[1]),
    ]
    for c in ends:
        c.start()
    for c in ends:
        c.wait()


def products(me, rows, cols, count, tiles, near, far, width):
    near, far = merged(near), merged(far)
    slots = tiles.shape[0]
    smem = pl.BlockSpec(memory_space=pltpu.SMEM)
    hbm = pl.BlockSpec(memory_space=pl.ANY)
    vmem = pl.BlockSpec(memory_space=pltpu.VMEM)
    partial = jax.ShapeDtypeStruct((4 * NX + 1, 256, width), jnp.float32)

    listed = jax.ShapeDtypeStruct((slots + BATCH,), jnp.int32)
    smem_list = pltpu.SMEM((slots + BATCH,), jnp.int32)

    def scratch(arrays, shards, *more):
        return [
            pltpu.VMEM((shards, 512, width), jnp.bfloat16),
            pltpu.VMEM(tiles.shape, jnp.bfloat16),
            *more,
            pltpu.SemaphoreType.DMA((sum(len(parts) for _, parts in arrays),)),
            pltpu.SemaphoreType.DMA((slots // BATCH,)),
        ]

    params = pltpu.CompilerParams(vmem_limit_bytes=VMEM_LIMIT)
    cost = pl.CostEstimate(flops=2 * slots * 256 * 256 * width, bytes_accessed=20 * 2**20, transcendentals=0)
    first, *lists = pl.pallas_call(
        functools.partial(near_kernel, [parts for _, parts in near]),
        out_shape=(partial, listed, listed, listed, jax.ShapeDtypeStruct((1,), jnp.int32)),
        in_specs=[smem] * 4 + [hbm] * (1 + len(near)),
        out_specs=(vmem, smem, smem, smem, smem),
        scratch_shapes=scratch(near, NZ * NY, smem_list, smem_list, smem_list),
        compiler_params=params,
        cost_estimate=cost,
    )(me, rows, cols, count, tiles, *[x for x, _ in near])
    half = jax.ShapeDtypeStruct((2 * NX, 256, width), jnp.float32)
    return pl.pallas_call(
        functools.partial(far_kernel, [parts for _, parts in far]),
        out_shape=(half, half),
        in_specs=[smem] * 4 + [hbm] * (2 + len(far)),
        out_specs=(hbm, hbm),
        scratch_shapes=scratch(far, 6, pltpu.VMEM(partial.shape, jnp.float32), pltpu.SemaphoreType.DMA((2,))),
        compiler_params=params,
    )(*lists, tiles, first, *[x for x, _ in far])


def dot_tn(a, b):
    return lax.dot_general(a, b, (((0,), (0,)), ((), ())), precision=HIGH, preferred_element_type=jnp.float32)


def dot_nt(a, b):
    return lax.dot_general(a, b, (((1,), (1,)), ((), ())), precision=HIGH, preferred_element_type=jnp.float32)


def dot_nn(a, b):
    return jnp.dot(a, b, precision=HIGH, preferred_element_type=jnp.float32)


def gram_kernel(total, me, p0, p1, p2, p3, panel, gram):
    p = (p0[...] + p1[...]) + (p2[...] + p3[...])
    panel[...] = p
    g = dot_tn(p, p) / total
    mx, mc = me[2], me[3]
    step = g.shape[0] // (2 * NX)
    for c in range(2):
        for x in range(NX):
            i = c * NX + x
            gram[c ^ mc, x ^ mx] = g[i * step : (i + 1) * step]


def factored(a, n):
    blocks = n // 8
    sub = lax.broadcasted_iota(jnp.int32, (8, n), 0)
    lane = lax.broadcasted_iota(jnp.int32, (8, n), 1)
    rows = [a[8 * i : 8 * i + 8] for i in range(blocks)]
    inv = [jnp.where(lane == sub + 8 * i, 1.0, 0.0).astype(jnp.float32) for i in range(blocks)]
    upper = []
    lower_inv = []

    def spread(x, k):
        return jnp.broadcast_to(x[k : k + 1, :], (8, n))

    for b in range(blocks):
        col = [
            {i: jnp.broadcast_to(rows[i][:, 8 * b + k : 8 * b + k + 1], (8, n)) for i in range(b, blocks)}
            for k in range(8)
        ]
        mult = []
        pivots = jnp.ones((8, n), jnp.float32)
        for k in range(8):
            d = spread(col[k][b], k)
            pivots = jnp.where(sub == k, d, pivots)
            rec = 1.0 / d
            m = {i: col[k][i] * rec for i in range(b, blocks)}
            m[b] = jnp.where(sub > k, m[b], 0.0)
            for j in range(k + 1, 8):
                u = spread(col[j][b], k)
                for i in range(b, blocks):
                    col[j][i] = col[j][i] - m[i] * u
            mult.append(m)
            rows[b] = rows[b] - m[b] * spread(rows[b], k)
            inv[b] = inv[b] - m[b] * spread(inv[b], k)
        for k in range(8):
            r, w = spread(rows[b], k), spread(inv[b], k)
            for i in range(b + 1, blocks):
                rows[i] = rows[i] - mult[k][i] * r
                inv[i] = inv[i] - mult[k][i] * w
        scale = lax.rsqrt(pivots)
        upper.append(jnp.where(lane >= sub + 8 * b, rows[b] * scale, 0.0))
        lower_inv.append(inv[b] * scale)
    return jnp.concatenate(upper), jnp.concatenate(lower_inv)


def finish_kernel(me, mine, theirs, panel, basis, factor, gram):
    mx, mc = me[2], me[3]
    step = gram.shape[0] // (2 * NX)
    for k in range(NX):
        own = mc * NX + (mx ^ k)
        far = (1 - mc) * NX + (mx ^ k)
        gram[pl.ds(pl.multiple_of(own * step, step), step)] = mine[k]
        gram[pl.ds(pl.multiple_of(far * step, step), step)] = theirs[k]
    h = gram.shape[0] // 2
    u1, w1 = factored(gram[:h, :h], h)
    l21 = dot_nt(gram[h:, :h], w1)
    u2, w2 = factored(gram[h:, h:] - dot_nt(l21, l21), h)
    q1 = dot_nt(panel[:, :h], w1)
    basis[:, :h] = q1
    basis[:, h:] = dot_nt(panel[:, h:] - dot_nt(q1, l21), w2)
    factor[:h, :h] = u1
    factor[:h, h:] = l21.T
    factor[h:, :h] = jnp.zeros((h, h), jnp.float32)
    factor[h:, h:] = u2


def on_device(vectors, tile_values, tile_row, tile_col, counts):
    slab, width = vectors.shape
    total = slab * lax.axis_size("row") * lax.axis_size("col")
    row, col = lax.axis_index("row"), lax.axis_index("col")
    me = jnp.stack([row // NY, row % NY, col // 2, col % 2]).astype(jnp.int32)
    smem = pl.BlockSpec(memory_space=pltpu.SMEM)
    vmem = pl.BlockSpec(memory_space=pltpu.VMEM)
    params = pltpu.CompilerParams(vmem_limit_bytes=24 * 2**20)

    near, far = stages(vectors)
    kept, sent = products(
        me, tile_row[0, 0], tile_col[0, 0], counts[0], tile_values[0, 0], near, far, width
    )
    pair = (kept + other_core(sent)).reshape(NX, slab, width)
    arrived = [from_x(pair[d], -d) for d in (1, 2, 3)]
    panel, gram = pl.pallas_call(
        functools.partial(gram_kernel, total),
        out_shape=(
            jax.ShapeDtypeStruct((slab, width), jnp.float32),
            jax.ShapeDtypeStruct((2, NX, width // (2 * NX), width), jnp.float32),
        ),
        in_specs=[smem] + [vmem] * 4,
        out_specs=(vmem, vmem),
        compiler_params=params,
    )(me, pair[0], *arrived)
    gram = gram[0] + other_core(gram[1])
    gram = (gram[0] + xor_x(gram[1], 1)) + (xor_x(gram[2], 2) + xor_x(gram[3], 3))
    gram = (gram + xor_y(gram, 1)) + (xor_y(gram, 2) + xor_y(gram, 3))
    for k in (1, 2, 4):
        gram = gram + xor_z(gram, k)
    mine = jnp.stack([gram] + [xor_x(gram, k) for k in range(1, NX)])
    theirs = other_core(mine)
    basis, factor = pl.pallas_call(
        finish_kernel,
        out_shape=(
            jax.ShapeDtypeStruct((slab, width), jnp.float32),
            jax.ShapeDtypeStruct((width, width), jnp.float32),
        ),
        in_specs=[smem] + [vmem] * 3,
        out_specs=(vmem, vmem),
        scratch_shapes=[pltpu.VMEM((width, width), jnp.float32)],
        compiler_params=params,
    )(me, mine, theirs, panel)
    return basis, factor


def solution(mesh):
    return jax.shard_map(
        on_device,
        mesh=mesh,
        in_specs=(
            P(("row", "col"), None),
            P("row", "col", None, None, None),
            P("row", "col", None),
            P("row", "col", None),
            P("row", "col"),
        ),
        out_specs=(P(("row", "col"), None), P()),
        check_vma=False,
    )
```

```python
import functools

import jax
import jax.numpy as jnp
from jax import lax
from jax.experimental import pallas as pl
from jax.experimental.pallas import tpu as pltpu
from jax.sharding import PartitionSpec as P

HIGH = lax.Precision.HIGHEST
NZ, NY, NX = 8, 4, 4
EARLY = 192
BATCH = 8
VMEM_LIMIT = 54 * 2**20


def from_y(a, d):
    return lax.ppermute(a, "row", [(z * NY + y, z * NY + (y - d) % NY) for z in range(NZ) for y in range(NY)])


def from_z(a, d):
    return lax.ppermute(a, "row", [(z * NY + y, (z - d) % NZ * NY + y) for z in range(NZ) for y in range(NY)])


def from_x(a, d):
    return lax.ppermute(a, "col", [(x * 2 + c, (x - d) % NX * 2 + c) for x in range(NX) for c in range(2)])


def xor_y(a, k):
    return lax.ppermute(a, "row", [(i, i ^ k) for i in range(NZ * NY)])


def xor_z(a, k):
    return lax.ppermute(a, "row", [(i, i ^ (k * NY)) for i in range(NZ * NY)])


def xor_x(a, k):
    return lax.ppermute(a, "col", [(i, i ^ (2 * k)) for i in range(2 * NX)])


def other_core(a):
    return lax.ppermute(a, "col", [(i, i ^ 1) for i in range(2 * NX)])


def stages(v, ids, lists, multiply):
    a, b = v[:EARLY], v[EARLY:]
    n = b.shape[0]
    h, w = n // 2, NY * EARLY
    together = lax.optimization_barrier
    join = jnp.concatenate

    def early(dz, dys=range(NY)):
        return [(i * EARLY, EARLY, dz, dy, 0) for i, dy in enumerate(dys)]

    def late(at, dz, dy):
        if dz < 5:
            return [(at, n, dz, dy, EARLY)]
        return [(at, h, dz, dy, EARLY + h), (at + h, h, dz, dy, EARLY)]

    def across(at, dzs, second):
        return [(at + i * h, h, dz, 2, EARLY + h * (second != (dz > 4))) for i, dz in enumerate(dzs)]

    def halves(x, count, second):
        return [x[i * n + h * second : i * n + h * second + h] for i in range(count)]

    ay1, ay3, bz1, bz7, ay2, ids = together(
        (from_y(a, 1), from_y(a, -1), from_z(b, 1), from_z(join([b[h:], b[:h]]), -1), from_y(a, 2), ids)
    )
    up1, down1 = join([a, ay1, ay2, ay3, bz1]), join([a, ay1, ay2, ay3, bz7])
    b0 = join([b, bz1, bz7])
    up2, down2, y1, y3, made = together(
        (from_z(up1, 1), from_z(down1, -1), from_y(b0, 1), from_y(b0, -1), lists(ids))
    )
    near = [(up1, early(0)), (up2, early(1)), (down2, early(7))]
    for x, dy in ((b0, 0), (y1, 1), (y3, 3)):
        near.append((x, [p for i, dz in enumerate((0, 1, 7)) for p in late(i * n, dz, dy)]))
    b1 = [up2[w:], down2[w:]]
    up3, down3, z1, z3, made = together(
        (
            from_z(up2, 1),
            from_z(down2, -1),
            from_y(join(b1 + halves(y1, 3, 0)), 1),
            from_y(join(b1 + halves(y3, 3, 1)), -1),
            made,
        )
    )
    near += [(up3, early(2)), (down3, early(6)), (up2, late(w, 2, 0)), (down2, late(w, 6, 0))]
    near += [
        (z1, late(0, 2, 1) + late(n, 6, 1) + across(2 * n, (0, 1, 7), 0)),
        (z3, late(0, 2, 3) + late(n, 6, 3) + across(2 * n, (0, 1, 7), 1)),
    ]
    b2 = [up3[w:], down3[w:]]
    near += [(up3, late(w, 3, 0)), (down3, late(w, 5, 0))]
    sums = multiply(0, made, (), near)
    up4, down4, y1, y3, made, sums = together(
        (
            from_z(up3[: w + h], 1),
            from_z(down3[: w + h], -1),
            from_y(join(b2 + halves(z1, 2, 0)), 1),
            from_y(join(b2 + halves(z3, 2, 1)), -1),
            made,
            sums,
        )
    )
    near += [(up4, early(3)), (down4, early(5))]
    near += [
        (y1, late(0, 3, 1) + late(n, 5, 1) + across(2 * n, (2, 6), 0)),
        (y3, late(0, 3, 3) + late(n, 5, 3) + across(2 * n, (2, 6), 1)),
    ]
    b4 = join([up4[w:], down4[w:]])
    sums = multiply(1, made, sums, near)
    up5, down5, z1, z3, z2, made, sums = together(
        (
            from_z(up4[: w // 2], 1),
            from_z(down4[w // 2 : w], -1),
            from_y(join([b4] + halves(y1, 2, 0)), 1),
            from_y(join([b4] + halves(y3, 2, 1)), -1),
            from_y(b4, 2),
            made,
            sums,
        )
    )
    near += [
        (up5, early(4, (0, 1))),
        (down5, early(4, (2, 3))),
        (b4, late(0, 4, 0)),
        (z1, late(0, 4, 1) + across(n, (3, 5), 0)),
        (z2, late(0, 4, 2)),
        (z3, late(0, 4, 3) + across(n, (3, 5), 1)),
    ]
    return multiply(2, made, sums, near)


def passes():
    codes = []
    used = [0, 0, 0]
    for dz in range(NZ):
        for dy in range(NY):
            off = min(dz, NZ - dz)
            p = 2 if off == 4 or (off == 3 and dy == 2) else 1 if off == 3 or (off == 2 and dy == 2) else 0
            codes.append(64 * p + used[p])
            used[p] += 1
    return codes, used


CODES, SHARDS = passes()


def of_pass(p, pieces):
    arrays = []
    for x, parts in pieces:
        mine = [
            (at, size, CODES[dz * NY + dy] % 64, first)
            for at, size, dz, dy, first in parts
            if CODES[dz * NY + dy] // 64 == p
        ]
        known = [has for y, has in arrays if y is x]
        if known:
            known[0].extend(mine)
        elif mine:
            arrays.append((x, mine))
    return arrays


def list_kernel(slots, me, rows, cols, count, codes, listed, shard, place, sizes):
    mz, my, mx, mc = me[0], me[1], me[2], me[3]
    for p in range(3):
        sizes[p] = 0

    def one(s, carry):
        part = cols[s]
        dz = (lax.shift_right_logical(part, 3) - mz) & (NZ - 1)
        dy = (lax.shift_right_logical(part, 1) - my) & (NY - 1)
        code = codes[dz * NY + dy]
        p = lax.shift_right_logical(code, 6)
        r = rows[s]
        c = lax.shift_right_logical(r, 1)
        dx = (lax.shift_right_logical(c, 1) - mx) & (NX - 1)
        n = sizes[p]
        sizes[p] = n + 1
        at = p * (slots + BATCH) + n
        listed[at] = s
        shard[at] = (code & 63) * 2 + (part & 1)
        place[at] = ((c & 1) ^ mc) * (2 * NX) + dx * 2 + (r & 1)
        return carry

    lax.fori_loop(0, count[0], one, 0)
    for p in range(3):
        for i in range(BATCH):
            at = p * (slots + BATCH) + sizes[p] + i
            listed[at] = 0
            shard[at] = 0
            place[at] = 4 * NX


def product_kernel(p, slots, places, widths, listed, shard, place, sizes, tiles, *refs):
    first = p == 0
    before = None if first else refs[0]
    refs = refs if first else refs[1:]
    n, m = len(places), len(widths)
    pieces, outs = refs[:n], refs[n : n + m]
    held, graph, total, sums, sems, tile_sems = refs[n + m :]
    base = p * (slots + BATCH)
    batches = (sizes[p] + BATCH - 1) // BATCH
    copies = []
    for parts, piece in zip(places, pieces, strict=True):
        for at, size, where, row in parts:
            to = held.at[where, pl.ds(row, size)]
            copies.append(pltpu.make_async_copy(piece.at[pl.ds(at, size)], to, sems.at[len(copies)]))
    if not first:
        copies.append(pltpu.make_async_copy(before, total.at[pl.ds(0, 4 * NX)], sums.at[0]))
    for c in copies:
        c.start()

    def fetch(b, carry):
        for i in range(BATCH):
            k = b * BATCH + i
            pltpu.make_async_copy(tiles.at[listed[base + k]], graph.at[k], tile_sems.at[b]).start()
        return carry

    lax.fori_loop(0, batches, fetch, 0)
    if first:
        total[...] = jnp.zeros_like(total)
    for c in copies:
        c.wait()

    def batch(b, carry):
        pltpu.make_async_copy(
            tiles.at[pl.ds(0, BATCH)], graph.at[pl.ds(b * BATCH, BATCH)], tile_sems.at[b]
        ).wait()
        for i in range(BATCH):
            k = b * BATCH + i
            part = shard[base + k]
            v = held[lax.shift_right_logical(part, 1), pl.ds(pl.multiple_of((part & 1) * 256, 256), 256), :]
            total[place[base + k]] += jnp.dot(graph[k], v, preferred_element_type=jnp.float32)
        return carry

    lax.fori_loop(0, batches, batch, 0)
    ends = []
    at = 4 * NX
    for i in reversed(range(m)):
        at -= widths[i]
        ends.append(pltpu.make_async_copy(total.at[pl.ds(at, widths[i])], outs[i], sums.at[i]))
    for c in ends:
        c.start()
    for c in ends:
        c.wait()


def listing(slots, ids, rows, cols, count):
    smem = pl.BlockSpec(memory_space=pltpu.SMEM)
    listed = jax.ShapeDtypeStruct((3 * (slots + BATCH),), jnp.int32)
    return pl.pallas_call(
        functools.partial(list_kernel, slots),
        out_shape=(listed, listed, listed, jax.ShapeDtypeStruct((3,), jnp.int32)),
        in_specs=[smem] * 5,
        out_specs=(smem,) * 4,
        cost_estimate=pl.CostEstimate(flops=2**31, bytes_accessed=2**12, transcendentals=0),
    )(ids, rows, cols, count, jnp.array(CODES, jnp.int32))


def product(tiles, width, p, lists, sums, pieces):
    slots = tiles.shape[0]
    smem = pl.BlockSpec(memory_space=pltpu.SMEM)
    hbm = pl.BlockSpec(memory_space=pl.ANY)
    arrays = of_pass(p, pieces)
    widths = (4 * NX,) if p < 2 else (2 * NX, 2 * NX)
    return pl.pallas_call(
        functools.partial(product_kernel, p, slots, [parts for _, parts in arrays], widths),
        out_shape=tuple(jax.ShapeDtypeStruct((n, 256, width), jnp.float32) for n in widths),
        in_specs=[smem] * 4 + [hbm] * (1 + len(sums) + len(arrays)),
        out_specs=(hbm,) * len(widths),
        scratch_shapes=[
            pltpu.VMEM((SHARDS[p], 512, width), jnp.bfloat16),
            pltpu.VMEM(tiles.shape, jnp.bfloat16),
            pltpu.VMEM((4 * NX + 1, 256, width), jnp.float32),
            pltpu.SemaphoreType.DMA((2,)),
            pltpu.SemaphoreType.DMA((sum(len(parts) for _, parts in arrays),)),
            pltpu.SemaphoreType.DMA((slots // BATCH,)),
        ],
        compiler_params=pltpu.CompilerParams(vmem_limit_bytes=VMEM_LIMIT),
        cost_estimate=pl.CostEstimate(
            flops=2 * slots * 256 * 256 * width * SHARDS[p] // (NZ * NY),
            bytes_accessed=(20 * SHARDS[p] // (NZ * NY) + 5) * 2**20,
            transcendentals=0,
        ),
    )(*lists, tiles, *sums, *[x for x, _ in arrays])


def dot_tn(a, b):
    return lax.dot_general(a, b, (((0,), (0,)), ((), ())), precision=HIGH, preferred_element_type=jnp.float32)


def dot_nt(a, b):
    return lax.dot_general(a, b, (((1,), (1,)), ((), ())), precision=HIGH, preferred_element_type=jnp.float32)


def dot_nn(a, b):
    return jnp.dot(a, b, precision=HIGH, preferred_element_type=jnp.float32)


def gram_kernel(total, me, p0, p1, p2, p3, panel, gram):
    p = (p0[...] + p1[...]) + (p2[...] + p3[...])
    panel[...] = p
    g = dot_tn(p, p) / total
    mx, mc = me[2], me[3]
    step = g.shape[0] // (2 * NX)
    for c in range(2):
        for x in range(NX):
            i = c * NX + x
            gram[c ^ mc, x ^ mx] = g[i * step : (i + 1) * step]


def factored(a, n):
    blocks = n // 8
    sub = lax.broadcasted_iota(jnp.int32, (8, n), 0)
    lane = lax.broadcasted_iota(jnp.int32, (8, n), 1)
    rows = [a[8 * i : 8 * i + 8] for i in range(blocks)]
    inv = [jnp.where(lane == sub + 8 * i, 1.0, 0.0).astype(jnp.float32) for i in range(blocks)]
    upper = []
    lower_inv = []

    def spread(x, k):
        return jnp.broadcast_to(x[k : k + 1, :], (8, n))

    for b in range(blocks):
        col = [
            {i: jnp.broadcast_to(rows[i][:, 8 * b + k : 8 * b + k + 1], (8, n)) for i in range(b, blocks)}
            for k in range(8)
        ]
        mult = []
        pivots = jnp.ones((8, n), jnp.float32)
        for k in range(8):
            d = spread(col[k][b], k)
            pivots = jnp.where(sub == k, d, pivots)
            rec = 1.0 / d
            m = {i: col[k][i] * rec for i in range(b, blocks)}
            m[b] = jnp.where(sub > k, m[b], 0.0)
            for j in range(k + 1, 8):
                u = spread(col[j][b], k)
                for i in range(b, blocks):
                    col[j][i] = col[j][i] - m[i] * u
            mult.append(m)
            rows[b] = rows[b] - m[b] * spread(rows[b], k)
            inv[b] = inv[b] - m[b] * spread(inv[b], k)
        for k in range(8):
            r, w = spread(rows[b], k), spread(inv[b], k)
            for i in range(b + 1, blocks):
                rows[i] = rows[i] - mult[k][i] * r
                inv[i] = inv[i] - mult[k][i] * w
        scale = lax.rsqrt(pivots)
        upper.append(jnp.where(lane >= sub + 8 * b, rows[b] * scale, 0.0))
        lower_inv.append(inv[b] * scale)
    return jnp.concatenate(upper), jnp.concatenate(lower_inv)


def finish_kernel(me, mine, theirs, panel, basis, factor, gram):
    mx, mc = me[2], me[3]
    step = gram.shape[0] // (2 * NX)
    for k in range(NX):
        own = mc * NX + (mx ^ k)
        far = (1 - mc) * NX + (mx ^ k)
        gram[pl.ds(pl.multiple_of(own * step, step), step)] = mine[k]
        gram[pl.ds(pl.multiple_of(far * step, step), step)] = theirs[k]
    h = gram.shape[0] // 2
    u1, w1 = factored(gram[:h, :h], h)
    l21 = dot_nt(gram[h:, :h], w1)
    u2, w2 = factored(gram[h:, h:] - dot_nt(l21, l21), h)
    q1 = dot_nt(panel[:, :h], w1)
    basis[:, :h] = q1
    basis[:, h:] = dot_nt(panel[:, h:] - dot_nt(q1, l21), w2)
    factor[:h, :h] = u1
    factor[:h, h:] = l21.T
    factor[h:, :h] = jnp.zeros((h, h), jnp.float32)
    factor[h:, h:] = u2


def on_device(vectors, tile_values, tile_row, tile_col, counts):
    slab, width = vectors.shape
    total = slab * lax.axis_size("row") * lax.axis_size("col")
    row, col = lax.axis_index("row"), lax.axis_index("col")
    me = jnp.stack([row // NY, row % NY, col // 2, col % 2]).astype(jnp.int32)
    smem = pl.BlockSpec(memory_space=pltpu.SMEM)
    vmem = pl.BlockSpec(memory_space=pltpu.VMEM)
    params = pltpu.CompilerParams(vmem_limit_bytes=24 * 2**20)

    tiles = tile_values[0, 0]
    kept, sent = stages(
        vectors,
        me,
        lambda ids: listing(tiles.shape[0], ids, tile_row[0, 0], tile_col[0, 0], counts[0]),
        functools.partial(product, tiles, width),
    )
    pair = (kept + other_core(sent)).reshape(NX, slab, width)
    arrived = [from_x(pair[d], -d) for d in (1, 2, 3)]
    panel, gram = pl.pallas_call(
        functools.partial(gram_kernel, total),
        out_shape=(
            jax.ShapeDtypeStruct((slab, width), jnp.float32),
            jax.ShapeDtypeStruct((2, NX, width // (2 * NX), width), jnp.float32),
        ),
        in_specs=[smem] + [vmem] * 4,
        out_specs=(vmem, vmem),
        compiler_params=params,
    )(me, pair[0], *arrived)
    gram = gram[0] + other_core(gram[1])
    gram = (gram[0] + xor_x(gram[1], 1)) + (xor_x(gram[2], 2) + xor_x(gram[3], 3))
    gram = (gram + xor_y(gram, 1)) + (xor_y(gram, 2) + xor_y(gram, 3))
    gram = gram + xor_z(gram, 1)
    gram = (gram + xor_z(gram, 2)) + (xor_z(gram, 4) + xor_z(gram, 6))
    mine = jnp.stack([gram] + [xor_x(gram, k) for k in range(1, NX)])
    theirs = other_core(mine)
    basis, factor = pl.pallas_call(
        finish_kernel,
        out_shape=(
            jax.ShapeDtypeStruct((slab, width), jnp.float32),
            jax.ShapeDtypeStruct((width, width), jnp.float32),
        ),
        in_specs=[smem] + [vmem] * 3,
        out_specs=(vmem, vmem),
        scratch_shapes=[pltpu.VMEM((width, width), jnp.float32)],
        compiler_params=params,
    )(me, mine, theirs, panel)
    return basis, factor


def solution(mesh):
    return jax.shard_map(
        on_device,
        mesh=mesh,
        in_specs=(
            P(("row", "col"), None),
            P("row", "col", None, None, None),
            P("row", "col", None),
            P("row", "col", None),
            P("row", "col"),
        ),
        out_specs=(P(("row", "col"), None), P()),
        check_vma=False,
    )
```

```python
import functools

import jax
import jax.numpy as jnp
from jax import lax
from jax.experimental import pallas as pl
from jax.experimental.pallas import tpu as pltpu
from jax.sharding import PartitionSpec as P

HIGH = lax.Precision.HIGHEST
NZ, NY, NX = 8, 4, 4
EARLY = 192
BATCH = 8
VMEM_LIMIT = 54 * 2**20
LAST_LIMIT = 40 * 2**20


def from_y(a, d):
    return lax.ppermute(a, "row", [(z * NY + y, z * NY + (y - d) % NY) for z in range(NZ) for y in range(NY)])


def from_z(a, d):
    return lax.ppermute(a, "row", [(z * NY + y, (z - d) % NZ * NY + y) for z in range(NZ) for y in range(NY)])


def from_x(a, d):
    return lax.ppermute(a, "col", [(x * 2 + c, (x - d) % NX * 2 + c) for x in range(NX) for c in range(2)])


def xor_y(a, k):
    return lax.ppermute(a, "row", [(i, i ^ k) for i in range(NZ * NY)])


def xor_z(a, k):
    return lax.ppermute(a, "row", [(i, i ^ (k * NY)) for i in range(NZ * NY)])


def xor_x(a, k):
    return lax.ppermute(a, "col", [(i, i ^ (2 * k)) for i in range(2 * NX)])


def other_core(a):
    return lax.ppermute(a, "col", [(i, i ^ 1) for i in range(2 * NX)])


def stages(v, ids, lists, multiply):
    a, b = v[:EARLY], v[EARLY:]
    n = b.shape[0]
    h, w = n // 2, NY * EARLY
    together = lax.optimization_barrier
    join = jnp.concatenate

    def early(dz, dys=range(NY)):
        return [(i * EARLY, EARLY, dz, dy, 0) for i, dy in enumerate(dys)]

    def late(at, dz, dy):
        if dz < 5:
            return [(at, n, dz, dy, EARLY)]
        return [(at, h, dz, dy, EARLY + h), (at + h, h, dz, dy, EARLY)]

    def across(at, dzs, second):
        return [(at + i * h, h, dz, 2, EARLY + h * (second != (dz > 4))) for i, dz in enumerate(dzs)]

    def halves(x, count, second):
        return [x[i * n + h * second : i * n + h * second + h] for i in range(count)]

    ay1, ay3, bz1, bz7, ay2, ids = together(
        (from_y(a, 1), from_y(a, -1), from_z(b, 1), from_z(join([b[h:], b[:h]]), -1), from_y(a, 2), ids)
    )
    up1, down1 = join([a, ay1, ay2, ay3, bz1]), join([a, ay1, ay2, ay3, bz7])
    b0 = join([b, bz1, bz7])
    up2, down2, y1, y3, made = together(
        (from_z(up1, 1), from_z(down1, -1), from_y(b0, 1), from_y(b0, -1), lists(ids))
    )
    near = [(up1, early(0)), (up2, early(1)), (down2, early(7))]
    for x, dy in ((b0, 0), (y1, 1), (y3, 3)):
        near.append((x, [p for i, dz in enumerate((0, 1, 7)) for p in late(i * n, dz, dy)]))
    b1 = [up2[w:], down2[w:]]
    up3, down3, z1, z3, made = together(
        (
            from_z(up2, 1),
            from_z(down2, -1),
            from_y(join(b1 + halves(y1, 3, 0)), 1),
            from_y(join(b1 + halves(y3, 3, 1)), -1),
            made,
        )
    )
    near += [(up3, early(2)), (down3, early(6)), (up2, late(w, 2, 0)), (down2, late(w, 6, 0))]
    near += [
        (z1, late(0, 2, 1) + late(n, 6, 1) + across(2 * n, (0, 1, 7), 0)),
        (z3, late(0, 2, 3) + late(n, 6, 3) + across(2 * n, (0, 1, 7), 1)),
    ]
    b2 = [up3[w:], down3[w:]]
    near += [(up3, late(w, 3, 0)), (down3, late(w, 5, 0))]
    sums = multiply(0, made, (), near)
    up4, down4, y1, y3, made, sums = together(
        (
            from_z(up3[: w + h], 1),
            from_z(down3[: w + h], -1),
            from_y(join(b2 + halves(z1, 2, 0)), 1),
            from_y(join(b2 + halves(z3, 2, 1)), -1),
            made,
            sums,
        )
    )
    near += [(x, [p for p in early(dz) if p[3] != 2]) for x, dz in ((up4, 3), (down4, 5))]
    near += [
        (y1, late(0, 3, 1) + late(n, 5, 1) + across(2 * n, (2, 6), 0)),
        (y3, late(0, 3, 3) + late(n, 5, 3) + across(2 * n, (2, 6), 1)),
    ]
    b4 = join([up4[w:], down4[w:]])
    sums = multiply(1, made, (sums,), near)
    up5, down5, z1, z3, z2, made, sums = together(
        (
            from_z(up4[: w // 2], 1),
            from_z(down4[w // 2 : w], -1),
            from_y(join([b4] + halves(y1, 2, 0)), 1),
            from_y(join([b4] + halves(y3, 2, 1)), -1),
            from_y(b4, 2),
            made,
            sums,
        )
    )
    near += [
        (up5, early(4, (0, 1))),
        (down5, early(4, (2, 3))),
        (b4, late(0, 4, 0)),
        (up4[2 * EARLY : 3 * EARLY], early(3, (2,))),
        (down4[2 * EARLY : 3 * EARLY], early(5, (2,))),
        (z1, late(0, 4, 1) + across(n, (3, 5), 0)),
        (z2, late(0, 4, 2)),
        (z3, late(0, 4, 3) + across(n, (3, 5), 1)),
    ]
    return multiply(2, made, (sums,), near)


def passes():
    codes = []
    used = [0, 0, 0]
    for dz in range(NZ):
        for dy in range(NY):
            off = min(dz, NZ - dz)
            p = 2 if off == 4 or (off == 3 and dy == 2) else 1 if off == 3 or (off == 2 and dy == 2) else 0
            codes.append(64 * p + used[p])
            used[p] += 1
    return codes, used


CODES, SHARDS = passes()


def of_pass(p, pieces):
    arrays = []
    for x, parts in pieces:
        mine = [
            (at, size, CODES[dz * NY + dy] % 64, first)
            for at, size, dz, dy, first in parts
            if CODES[dz * NY + dy] // 64 == p
        ]
        known = [has for y, has in arrays if y is x]
        if known:
            known[0].extend(mine)
        elif mine:
            arrays.append((x, mine))
    return arrays


def list_kernel(slots, me, rows, cols, count, codes, listed, shard, place, sizes):
    mz, my, mx, mc = me[0], me[1], me[2], me[3]
    for p in range(3):
        sizes[p] = 0

    def one(s, carry):
        part = cols[s]
        dz = (lax.shift_right_logical(part, 3) - mz) & (NZ - 1)
        dy = (lax.shift_right_logical(part, 1) - my) & (NY - 1)
        code = codes[dz * NY + dy]
        p = lax.shift_right_logical(code, 6)
        r = rows[s]
        c = lax.shift_right_logical(r, 1)
        dx = (lax.shift_right_logical(c, 1) - mx) & (NX - 1)
        n = sizes[p]
        sizes[p] = n + 1
        at = p * (slots + BATCH) + n
        listed[at] = s
        shard[at] = (code & 63) * 2 + (part & 1)
        place[at] = ((c & 1) ^ mc) * (2 * NX) + dx * 2 + (r & 1)
        return carry

    lax.fori_loop(0, count[0], one, 0)
    for p in range(3):
        for i in range(BATCH):
            at = p * (slots + BATCH) + sizes[p] + i
            listed[at] = 0
            shard[at] = 0
            place[at] = 4 * NX


def product_kernel(p, slots, places, listed, shard, place, sizes, tiles, *refs):
    first = p == 0
    before = None if first else refs[0]
    refs = refs if first else refs[1:]
    n, last = len(places), p > 0
    pieces, out = refs[:n], refs[n]
    total = out if last else refs[n + 1]
    held, graph, sums, sems, tile_sems = refs[n + 2 - last :]
    base = p * (slots + BATCH)
    batches = (sizes[p] + BATCH - 1) // BATCH
    copies = []
    for parts, piece in zip(places, pieces, strict=True):
        for at, size, where, row in parts:
            to = held.at[where, pl.ds(row, size)]
            copies.append(pltpu.make_async_copy(piece.at[pl.ds(at, size)], to, sems.at[len(copies)]))
    for c in copies:
        c.start()

    def fetch(b, carry):
        for i in range(BATCH):
            k = b * BATCH + i
            pltpu.make_async_copy(tiles.at[listed[base + k]], graph.at[k], tile_sems.at[b]).start()
        return carry

    lax.fori_loop(0, batches, fetch, 0)
    if first:
        total[...] = jnp.zeros_like(total)
    if last:
        total[: 4 * NX] = before[: 4 * NX]
        total[4 * NX] = jnp.zeros(total.shape[1:], jnp.float32)
    for c in copies:
        c.wait()

    def batch(b, carry):
        pltpu.make_async_copy(
            tiles.at[pl.ds(0, BATCH)], graph.at[pl.ds(b * BATCH, BATCH)], tile_sems.at[b]
        ).wait()
        for i in range(BATCH):
            k = b * BATCH + i
            part = shard[base + k]
            v = held[lax.shift_right_logical(part, 1), pl.ds(pl.multiple_of((part & 1) * 256, 256), 256), :]
            total[place[base + k]] += jnp.dot(graph[k], v, preferred_element_type=jnp.float32)
        return carry

    lax.fori_loop(0, batches, batch, 0)
    if not last:
        end = pltpu.make_async_copy(total.at[pl.ds(0, 4 * NX)], out, sums.at[0])
        end.start()
        end.wait()


def listing(slots, ids, rows, cols, count):
    smem = pl.BlockSpec(memory_space=pltpu.SMEM)
    listed = jax.ShapeDtypeStruct((3 * (slots + BATCH),), jnp.int32)
    return pl.pallas_call(
        functools.partial(list_kernel, slots),
        out_shape=(listed, listed, listed, jax.ShapeDtypeStruct((3,), jnp.int32)),
        in_specs=[smem] * 5,
        out_specs=(smem,) * 4,
        cost_estimate=pl.CostEstimate(flops=2**31, bytes_accessed=2**12, transcendentals=0),
    )(ids, rows, cols, count, jnp.array(CODES, jnp.int32))


def product(tiles, width, p, lists, sums, pieces):
    slots = tiles.shape[0]
    smem = pl.BlockSpec(memory_space=pltpu.SMEM)
    hbm = pl.BlockSpec(memory_space=pl.ANY)
    vmem = pl.BlockSpec(memory_space=pltpu.VMEM)
    arrays = of_pass(p, pieces)
    last = p > 0
    partial = (4 * NX + last, 256, width)
    return pl.pallas_call(
        functools.partial(product_kernel, p, slots, [parts for _, parts in arrays]),
        out_shape=jax.ShapeDtypeStruct(partial, jnp.float32),
        in_specs=[smem] * 4 + [hbm] + [vmem if last else hbm] * len(sums) + [hbm] * len(arrays),
        out_specs=vmem if last else hbm,
        scratch_shapes=[
            *([] if last else [pltpu.VMEM((4 * NX + 1, 256, width), jnp.float32)]),
            pltpu.VMEM((SHARDS[p], 512, width), jnp.bfloat16),
            pltpu.VMEM(tiles.shape, jnp.bfloat16),
            pltpu.SemaphoreType.DMA((1,)),
            pltpu.SemaphoreType.DMA((sum(len(parts) for _, parts in arrays),)),
            pltpu.SemaphoreType.DMA((slots // BATCH,)),
        ],
        compiler_params=pltpu.CompilerParams(vmem_limit_bytes=LAST_LIMIT if last else VMEM_LIMIT),
        cost_estimate=pl.CostEstimate(
            flops=2 * slots * 256 * 256 * width * SHARDS[p] // (NZ * NY),
            bytes_accessed=(20 * SHARDS[p] // (NZ * NY) + 5) * 2**20,
            transcendentals=0,
        ),
    )(*lists, tiles, *sums, *[x for x, _ in arrays])


def dot_tn(a, b):
    return lax.dot_general(a, b, (((0,), (0,)), ((), ())), precision=HIGH, preferred_element_type=jnp.float32)


def dot_nt(a, b):
    return lax.dot_general(a, b, (((1,), (1,)), ((), ())), precision=HIGH, preferred_element_type=jnp.float32)


def dot_nn(a, b):
    return jnp.dot(a, b, precision=HIGH, preferred_element_type=jnp.float32)


def gram_kernel(total, me, p0, p1, p2, p3, panel, gram):
    p = (p0[...] + p1[...]) + (p2[...] + p3[...])
    panel[...] = p
    g = dot_tn(p, p) / total
    mx, mc = me[2], me[3]
    step = g.shape[0] // (2 * NX)
    for c in range(2):
        for x in range(NX):
            i = c * NX + x
            gram[c ^ mc, x ^ mx] = g[i * step : (i + 1) * step]


def factored(a, n):
    blocks = n // 8
    sub = lax.broadcasted_iota(jnp.int32, (8, n), 0)
    lane = lax.broadcasted_iota(jnp.int32, (8, n), 1)
    rows = [a[8 * i : 8 * i + 8] for i in range(blocks)]
    inv = [jnp.where(lane == sub + 8 * i, 1.0, 0.0).astype(jnp.float32) for i in range(blocks)]
    upper = []
    lower_inv = []

    def spread(x, k):
        return jnp.broadcast_to(x[k : k + 1, :], (8, n))

    for b in range(blocks):
        col = [
            {i: jnp.broadcast_to(rows[i][:, 8 * b + k : 8 * b + k + 1], (8, n)) for i in range(b, blocks)}
            for k in range(8)
        ]
        mult = []
        pivots = jnp.ones((8, n), jnp.float32)
        for k in range(8):
            d = spread(col[k][b], k)
            pivots = jnp.where(sub == k, d, pivots)
            rec = 1.0 / d
            m = {i: col[k][i] * rec for i in range(b, blocks)}
            m[b] = jnp.where(sub > k, m[b], 0.0)
            for j in range(k + 1, 8):
                u = spread(col[j][b], k)
                for i in range(b, blocks):
                    col[j][i] = col[j][i] - m[i] * u
            mult.append(m)
            rows[b] = rows[b] - m[b] * spread(rows[b], k)
            inv[b] = inv[b] - m[b] * spread(inv[b], k)
        for k in range(8):
            r, w = spread(rows[b], k), spread(inv[b], k)
            for i in range(b + 1, blocks):
                rows[i] = rows[i] - mult[k][i] * r
                inv[i] = inv[i] - mult[k][i] * w
        scale = lax.rsqrt(pivots)
        upper.append(jnp.where(lane >= sub + 8 * b, rows[b] * scale, 0.0))
        lower_inv.append(inv[b] * scale)
    return jnp.concatenate(upper), jnp.concatenate(lower_inv)


def finish_kernel(me, mine, theirs, panel, basis, factor, gram):
    mx, mc = me[2], me[3]
    step = gram.shape[0] // (2 * NX)
    for k in range(NX):
        own = mc * NX + (mx ^ k)
        far = (1 - mc) * NX + (mx ^ k)
        gram[pl.ds(pl.multiple_of(own * step, step), step)] = mine[k]
        gram[pl.ds(pl.multiple_of(far * step, step), step)] = theirs[k]
    h = gram.shape[0] // 2
    u1, w1 = factored(gram[:h, :h], h)
    l21 = dot_nt(gram[h:, :h], w1)
    u2, w2 = factored(gram[h:, h:] - dot_nt(l21, l21), h)
    q1 = dot_nt(panel[:, :h], w1)
    basis[:, :h] = q1
    basis[:, h:] = dot_nt(panel[:, h:] - dot_nt(q1, l21), w2)
    factor[:h, :h] = u1
    factor[:h, h:] = l21.T
    factor[h:, :h] = jnp.zeros((h, h), jnp.float32)
    factor[h:, h:] = u2


def on_device(vectors, tile_values, tile_row, tile_col, counts):
    slab, width = vectors.shape
    total = slab * lax.axis_size("row") * lax.axis_size("col")
    row, col = lax.axis_index("row"), lax.axis_index("col")
    me = jnp.stack([row // NY, row % NY, col // 2, col % 2]).astype(jnp.int32)
    smem = pl.BlockSpec(memory_space=pltpu.SMEM)
    vmem = pl.BlockSpec(memory_space=pltpu.VMEM)
    params = pltpu.CompilerParams(vmem_limit_bytes=24 * 2**20)

    tiles = tile_values[0, 0]
    parts = stages(
        vectors,
        me,
        lambda ids: listing(tiles.shape[0], ids, tile_row[0, 0], tile_col[0, 0], counts[0]),
        functools.partial(product, tiles, width),
    )
    pair = (parts[: 2 * NX] + other_core(parts[2 * NX : 4 * NX])).reshape(NX, slab, width)
    arrived = [from_x(pair[d], -d) for d in (1, 2, 3)]
    panel, gram = pl.pallas_call(
        functools.partial(gram_kernel, total),
        out_shape=(
            jax.ShapeDtypeStruct((slab, width), jnp.float32),
            jax.ShapeDtypeStruct((2, NX, width // (2 * NX), width), jnp.float32),
        ),
        in_specs=[smem] + [vmem] * 4,
        out_specs=(vmem, vmem),
        compiler_params=params,
    )(me, pair[0], *arrived)
    gram = gram[0] + other_core(gram[1])
    gram = (gram[0] + xor_x(gram[1], 1)) + (xor_x(gram[2], 2) + xor_x(gram[3], 3))
    gram = (gram + xor_y(gram, 1)) + (xor_y(gram, 2) + xor_y(gram, 3))
    gram = gram + xor_z(gram, 1)
    gram = (gram + xor_z(gram, 2)) + (xor_z(gram, 4) + xor_z(gram, 6))
    mine = jnp.stack([gram] + [xor_x(gram, k) for k in range(1, NX)])
    theirs = other_core(mine)
    basis, factor = pl.pallas_call(
        finish_kernel,
        out_shape=(
            jax.ShapeDtypeStruct((slab, width), jnp.float32),
            jax.ShapeDtypeStruct((width, width), jnp.float32),
        ),
        in_specs=[smem] + [vmem] * 3,
        out_specs=(vmem, vmem),
        scratch_shapes=[pltpu.VMEM((width, width), jnp.float32)],
        compiler_params=params,
    )(me, mine, theirs, panel)
    return basis, factor


def solution(mesh):
    return jax.shard_map(
        on_device,
        mesh=mesh,
        in_specs=(
            P(("row", "col"), None),
            P("row", "col", None, None, None),
            P("row", "col", None),
            P("row", "col", None),
            P("row", "col"),
        ),
        out_specs=(P(("row", "col"), None), P()),
        check_vma=False,
    )
```

```python
import functools

import jax
import jax.numpy as jnp
from jax import lax
from jax.experimental import pallas as pl
from jax.experimental.pallas import tpu as pltpu
from jax.sharding import PartitionSpec as P

HIGH = lax.Precision.HIGHEST
NZ, NY, NX = 8, 4, 4
EARLY = 192
BATCH = 8
VMEM_LIMIT = 54 * 2**20
LAST_LIMIT = 40 * 2**20


def from_y(a, d):
    return lax.ppermute(a, "row", [(z * NY + y, z * NY + (y - d) % NY) for z in range(NZ) for y in range(NY)])


def from_z(a, d):
    return lax.ppermute(a, "row", [(z * NY + y, (z - d) % NZ * NY + y) for z in range(NZ) for y in range(NY)])


def from_x(a, d):
    return lax.ppermute(a, "col", [(x * 2 + c, (x - d) % NX * 2 + c) for x in range(NX) for c in range(2)])


def xor_y(a, k):
    return lax.ppermute(a, "row", [(i, i ^ k) for i in range(NZ * NY)])


def xor_z(a, k):
    return lax.ppermute(a, "row", [(i, i ^ (k * NY)) for i in range(NZ * NY)])


def xor_x(a, k):
    return lax.ppermute(a, "col", [(i, i ^ (2 * k)) for i in range(2 * NX)])


def other_core(a):
    return lax.ppermute(a, "col", [(i, i ^ 1) for i in range(2 * NX)])


def stages(v, ids, lists, multiply):
    a, b = v[:EARLY], v[EARLY:]
    n = b.shape[0]
    h, w = n // 2, NY * EARLY
    together = lax.optimization_barrier
    join = jnp.concatenate

    def early(dz, dys=range(NY)):
        return [(i * EARLY, EARLY, dz, dy, 0) for i, dy in enumerate(dys)]

    def late(at, dz, dy):
        if dz < 5:
            return [(at, n, dz, dy, EARLY)]
        return [(at, h, dz, dy, EARLY + h), (at + h, h, dz, dy, EARLY)]

    def across(at, dzs, second):
        return [(at + i * h, h, dz, 2, EARLY + h * (second != (dz > 4))) for i, dz in enumerate(dzs)]

    def halves(x, count, second):
        return [x[i * n + h * second : i * n + h * second + h] for i in range(count)]

    ay1, ay3, bz1, bz7, ay2, ids = together(
        (from_y(a, 1), from_y(a, -1), from_z(b, 1), from_z(join([b[h:], b[:h]]), -1), from_y(a, 2), ids)
    )
    up1, down1 = join([a, ay1, ay2, ay3, bz1]), join([a, ay1, ay2, ay3, bz7])
    b0 = join([b, bz1, bz7])
    up2, down2, y1, y3, made = together(
        (from_z(up1, 1), from_z(down1, -1), from_y(b0, 1), from_y(b0, -1), lists(ids))
    )
    near = [(up1, early(0)), (up2, early(1)), (down2, early(7))]
    for x, dy in ((b0, 0), (y1, 1), (y3, 3)):
        near.append((x, [p for i, dz in enumerate((0, 1, 7)) for p in late(i * n, dz, dy)]))
    b1 = [up2[w:], down2[w:]]
    up3, down3, z1, z3, made = together(
        (
            from_z(up2, 1),
            from_z(down2, -1),
            from_y(join(b1 + halves(y1, 3, 0)), 1),
            from_y(join(b1 + halves(y3, 3, 1)), -1),
            made,
        )
    )
    near += [(up3, early(2)), (down3, early(6)), (up2, late(w, 2, 0)), (down2, late(w, 6, 0))]
    near += [
        (z1, late(0, 2, 1) + late(n, 6, 1) + across(2 * n, (0, 1, 7), 0)),
        (z3, late(0, 2, 3) + late(n, 6, 3) + across(2 * n, (0, 1, 7), 1)),
    ]
    b2 = [up3[w:], down3[w:]]
    near += [(up3, late(w, 3, 0)), (down3, late(w, 5, 0))]
    sums = multiply(0, made, (), near)
    up4, down4, y1, y3, made, sums = together(
        (
            from_z(up3[: w + h], 1),
            from_z(down3[: w + h], -1),
            from_y(join(b2 + halves(z1, 2, 0)), 1),
            from_y(join(b2 + halves(z3, 2, 1)), -1),
            made,
            sums,
        )
    )
    near += [(x, [p for p in early(dz) if p[3] != 2]) for x, dz in ((up4, 3), (down4, 5))]
    near += [
        (y1, late(0, 3, 1) + late(n, 5, 1) + across(2 * n, (2, 6), 0)),
        (y3, late(0, 3, 3) + late(n, 5, 3) + across(2 * n, (2, 6), 1)),
    ]
    b4 = join([up4[w:], down4[w:]])
    sums = multiply(1, made, (sums,), near)
    up5, down5, z1, z3, z2, made, sums = together(
        (
            from_z(up4[: w // 2], 1),
            from_z(down4[w // 2 : w], -1),
            from_y(join([b4] + halves(y1, 2, 0)), 1),
            from_y(join([b4] + halves(y3, 2, 1)), -1),
            from_y(b4, 2),
            made,
            sums,
        )
    )
    near += [
        (up5, early(4, (0, 1))),
        (down5, early(4, (2, 3))),
        (b4, late(0, 4, 0)),
        (up4[2 * EARLY : 3 * EARLY], early(3, (2,))),
        (down4[2 * EARLY : 3 * EARLY], early(5, (2,))),
        (z1, late(0, 4, 1) + across(n, (3, 5), 0)),
        (z2, late(0, 4, 2)),
        (z3, late(0, 4, 3) + across(n, (3, 5), 1)),
    ]
    return multiply(2, made, (sums,), near)


def passes():
    codes = []
    used = [0, 0, 0]
    for dz in range(NZ):
        for dy in range(NY):
            off = min(dz, NZ - dz)
            p = 2 if off == 4 or (off == 3 and dy == 2) else 1 if off == 3 or (off == 2 and dy == 2) else 0
            codes.append(64 * p + used[p])
            used[p] += 1
    return codes, used


CODES, SHARDS = passes()


def of_pass(p, pieces):
    arrays = []
    for x, parts in pieces:
        mine = [
            (at, size, CODES[dz * NY + dy] % 64, first)
            for at, size, dz, dy, first in parts
            if CODES[dz * NY + dy] // 64 == p
        ]
        known = [has for y, has in arrays if y is x]
        if known:
            known[0].extend(mine)
        elif mine:
            arrays.append((x, mine))
    return arrays


def list_kernel(slots, me, rows, cols, count, codes, listed, shard, place, sizes):
    mz, my, mx, mc = me[0], me[1], me[2], me[3]
    for p in range(3):
        sizes[p] = 0

    def one(s, carry):
        part = cols[s]
        dz = (lax.shift_right_logical(part, 3) - mz) & (NZ - 1)
        dy = (lax.shift_right_logical(part, 1) - my) & (NY - 1)
        code = codes[dz * NY + dy]
        p = lax.shift_right_logical(code, 6)
        r = rows[s]
        c = lax.shift_right_logical(r, 1)
        dx = (lax.shift_right_logical(c, 1) - mx) & (NX - 1)
        n = sizes[p]
        sizes[p] = n + 1
        at = p * (slots + BATCH) + n
        listed[at] = s
        shard[at] = (code & 63) * 2 + (part & 1)
        place[at] = ((c & 1) ^ mc) * (2 * NX) + dx * 2 + (r & 1)
        return carry

    lax.fori_loop(0, count[0], one, 0)
    for p in range(3):
        for i in range(BATCH):
            at = p * (slots + BATCH) + sizes[p] + i
            listed[at] = 0
            shard[at] = 0
            place[at] = 4 * NX


def product_kernel(p, slots, places, listed, shard, place, sizes, tiles, *refs):
    first = p == 0
    before = None if first else refs[0]
    refs = refs if first else refs[1:]
    n, last = len(places), p > 0
    pieces, out = refs[:n], refs[n]
    total = out if last else refs[n + 1]
    held, graph, sums, sems, tile_sems = refs[n + 2 - last :]
    base = p * (slots + BATCH)
    batches = (sizes[p] + BATCH - 1) // BATCH
    copies = []
    for parts, piece in zip(places, pieces, strict=True):
        for at, size, where, row in parts:
            to = held.at[where, pl.ds(row, size)]
            copies.append(pltpu.make_async_copy(piece.at[pl.ds(at, size)], to, sems.at[len(copies)]))
    for c in copies:
        c.start()

    def fetch(b, carry):
        for i in range(BATCH):
            k = b * BATCH + i
            pltpu.make_async_copy(tiles.at[listed[base + k]], graph.at[k], tile_sems.at[b]).start()
        return carry

    lax.fori_loop(0, batches, fetch, 0)
    if first:
        total[...] = jnp.zeros_like(total)
    if last:
        total[: 4 * NX] = before[: 4 * NX]
        total[4 * NX] = jnp.zeros(total.shape[1:], jnp.float32)
    for c in copies:
        c.wait()

    def batch(b, carry):
        pltpu.make_async_copy(
            tiles.at[pl.ds(0, BATCH)], graph.at[pl.ds(b * BATCH, BATCH)], tile_sems.at[b]
        ).wait()
        for i in range(BATCH):
            k = b * BATCH + i
            part = shard[base + k]
            v = held[lax.shift_right_logical(part, 1), pl.ds(pl.multiple_of((part & 1) * 256, 256), 256), :]
            total[place[base + k]] += jnp.dot(graph[k], v, preferred_element_type=jnp.float32)
        return carry

    lax.fori_loop(0, batches, batch, 0)
    if not last:
        end = pltpu.make_async_copy(total.at[pl.ds(0, 4 * NX)], out, sums.at[0])
        end.start()
        end.wait()


def listing(slots, ids, rows, cols, count):
    smem = pl.BlockSpec(memory_space=pltpu.SMEM)
    listed = jax.ShapeDtypeStruct((3 * (slots + BATCH),), jnp.int32)
    return pl.pallas_call(
        functools.partial(list_kernel, slots),
        out_shape=(listed, listed, listed, jax.ShapeDtypeStruct((3,), jnp.int32)),
        in_specs=[smem] * 5,
        out_specs=(smem,) * 4,
        cost_estimate=pl.CostEstimate(flops=2**31, bytes_accessed=2**12, transcendentals=0),
    )(ids, rows, cols, count, jnp.array(CODES, jnp.int32))


def product(tiles, width, p, lists, sums, pieces):
    slots = tiles.shape[0]
    smem = pl.BlockSpec(memory_space=pltpu.SMEM)
    hbm = pl.BlockSpec(memory_space=pl.ANY)
    vmem = pl.BlockSpec(memory_space=pltpu.VMEM)
    arrays = of_pass(p, pieces)
    last = p > 0
    partial = (4 * NX + last, 256, width)
    return pl.pallas_call(
        functools.partial(product_kernel, p, slots, [parts for _, parts in arrays]),
        out_shape=jax.ShapeDtypeStruct(partial, jnp.float32),
        in_specs=[smem] * 4 + [hbm] + [vmem if last else hbm] * len(sums) + [hbm] * len(arrays),
        out_specs=vmem if last else hbm,
        scratch_shapes=[
            *([] if last else [pltpu.VMEM((4 * NX + 1, 256, width), jnp.float32)]),
            pltpu.VMEM((SHARDS[p], 512, width), jnp.bfloat16),
            pltpu.VMEM(tiles.shape, jnp.bfloat16),
            pltpu.SemaphoreType.DMA((1,)),
            pltpu.SemaphoreType.DMA((sum(len(parts) for _, parts in arrays),)),
            pltpu.SemaphoreType.DMA((slots // BATCH,)),
        ],
        compiler_params=pltpu.CompilerParams(vmem_limit_bytes=LAST_LIMIT if last else VMEM_LIMIT),
        cost_estimate=pl.CostEstimate(
            flops=2 * slots * 256 * 256 * width * SHARDS[p] // (NZ * NY),
            bytes_accessed=(20 * SHARDS[p] // (NZ * NY) + 5) * 2**20,
            transcendentals=0,
        ),
    )(*lists, tiles, *sums, *[x for x, _ in arrays])


def dot_tn(a, b):
    return lax.dot_general(a, b, (((0,), (0,)), ((), ())), precision=HIGH, preferred_element_type=jnp.float32)


def dot_nt(a, b):
    return lax.dot_general(a, b, (((1,), (1,)), ((), ())), precision=HIGH, preferred_element_type=jnp.float32)


def dot_nn(a, b):
    return jnp.dot(a, b, precision=HIGH, preferred_element_type=jnp.float32)


def gram_kernel(total, me, own, r1, r3, q1, q3, panel, gram):
    h = own.shape[0] // 2
    p = jnp.concatenate([own[:h] + r3[h:] + q1[...], own[h:] + r1[h:] + q3[...]])
    panel[...] = p
    g = dot_tn(p, p) / total
    mx, mc = me[2], me[3]
    step = g.shape[0] // (2 * NX)
    for c in range(2):
        for x in range(NX):
            i = c * NX + x
            gram[c ^ mc, x ^ mx] = g[i * step : (i + 1) * step]


def factored(a, n):
    blocks = n // 8
    sub = lax.broadcasted_iota(jnp.int32, (8, n), 0)
    lane = lax.broadcasted_iota(jnp.int32, (8, n), 1)
    rows = [a[8 * i : 8 * i + 8] for i in range(blocks)]
    inv = [jnp.where(lane == sub + 8 * i, 1.0, 0.0).astype(jnp.float32) for i in range(blocks)]
    upper = []
    lower_inv = []

    def spread(x, k):
        return jnp.broadcast_to(x[k : k + 1, :], (8, n))

    for b in range(blocks):
        col = [
            {i: jnp.broadcast_to(rows[i][:, 8 * b + k : 8 * b + k + 1], (8, n)) for i in range(b, blocks)}
            for k in range(8)
        ]
        mult = []
        pivots = jnp.ones((8, n), jnp.float32)
        for k in range(8):
            d = spread(col[k][b], k)
            pivots = jnp.where(sub == k, d, pivots)
            rec = 1.0 / d
            m = {i: col[k][i] * rec for i in range(b, blocks)}
            m[b] = jnp.where(sub > k, m[b], 0.0)
            for j in range(k + 1, 8):
                u = spread(col[j][b], k)
                for i in range(b, blocks):
                    col[j][i] = col[j][i] - m[i] * u
            mult.append(m)
            rows[b] = rows[b] - m[b] * spread(rows[b], k)
            inv[b] = inv[b] - m[b] * spread(inv[b], k)
        for k in range(8):
            r, w = spread(rows[b], k), spread(inv[b], k)
            for i in range(b + 1, blocks):
                rows[i] = rows[i] - mult[k][i] * r
                inv[i] = inv[i] - mult[k][i] * w
        scale = lax.rsqrt(pivots)
        upper.append(jnp.where(lane >= sub + 8 * b, rows[b] * scale, 0.0))
        lower_inv.append(inv[b] * scale)
    return jnp.concatenate(upper), jnp.concatenate(lower_inv)


def finish_kernel(me, mine, theirs, panel, basis, factor, gram):
    mx, mc = me[2], me[3]
    step = gram.shape[0] // (2 * NX)
    for k in range(NX):
        own = mc * NX + (mx ^ k)
        far = (1 - mc) * NX + (mx ^ k)
        gram[pl.ds(pl.multiple_of(own * step, step), step)] = mine[k]
        gram[pl.ds(pl.multiple_of(far * step, step), step)] = theirs[k]
    h = gram.shape[0] // 2
    u1, w1 = factored(gram[:h, :h], h)
    l21 = dot_nt(gram[h:, :h], w1)
    u2, w2 = factored(gram[h:, h:] - dot_nt(l21, l21), h)
    q1 = dot_nt(panel[:, :h], w1)
    basis[:, :h] = q1
    basis[:, h:] = dot_nt(panel[:, h:] - dot_nt(q1, l21), w2)
    factor[:h, :h] = u1
    factor[:h, h:] = l21.T
    factor[h:, :h] = jnp.zeros((h, h), jnp.float32)
    factor[h:, h:] = u2


def on_device(vectors, tile_values, tile_row, tile_col, counts):
    slab, width = vectors.shape
    total = slab * lax.axis_size("row") * lax.axis_size("col")
    row, col = lax.axis_index("row"), lax.axis_index("col")
    me = jnp.stack([row // NY, row % NY, col // 2, col % 2]).astype(jnp.int32)
    smem = pl.BlockSpec(memory_space=pltpu.SMEM)
    vmem = pl.BlockSpec(memory_space=pltpu.VMEM)
    params = pltpu.CompilerParams(vmem_limit_bytes=24 * 2**20)

    tiles = tile_values[0, 0]
    parts = stages(
        vectors,
        me,
        lambda ids: listing(tiles.shape[0], ids, tile_row[0, 0], tile_col[0, 0], counts[0]),
        functools.partial(product, tiles, width),
    )
    pair = (parts[: 2 * NX] + other_core(parts[2 * NX : 4 * NX])).reshape(NX, slab, width)
    h = slab // 2
    r1 = from_x(jnp.concatenate([pair[2, :h], pair[1, h:]]), -1)
    r3 = from_x(jnp.concatenate([pair[2, h:], pair[3, :h]]), 1)
    q1 = from_x(pair[1, :h] + r1[:h], -1)
    q3 = from_x(pair[3, h:] + r3[:h], 1)
    panel, gram = pl.pallas_call(
        functools.partial(gram_kernel, total),
        out_shape=(
            jax.ShapeDtypeStruct((slab, width), jnp.float32),
            jax.ShapeDtypeStruct((2, NX, width // (2 * NX), width), jnp.float32),
        ),
        in_specs=[smem] + [vmem] * 5,
        out_specs=(vmem, vmem),
        compiler_params=params,
    )(me, pair[0], r1, r3, q1, q3)
    gram = gram[0] + other_core(gram[1])
    gram = (gram[0] + xor_x(gram[1], 1)) + (xor_x(gram[2], 2) + xor_x(gram[3], 3))
    gram = (gram + xor_y(gram, 1)) + (xor_y(gram, 2) + xor_y(gram, 3))
    gram = gram + xor_z(gram, 1)
    gram = (gram + xor_z(gram, 2)) + (xor_z(gram, 4) + xor_z(gram, 6))
    mine = jnp.stack([gram] + [xor_x(gram, k) for k in range(1, NX)])
    theirs = other_core(mine)
    basis, factor = pl.pallas_call(
        finish_kernel,
        out_shape=(
            jax.ShapeDtypeStruct((slab, width), jnp.float32),
            jax.ShapeDtypeStruct((width, width), jnp.float32),
        ),
        in_specs=[smem] + [vmem] * 3,
        out_specs=(vmem, vmem),
        scratch_shapes=[pltpu.VMEM((width, width), jnp.float32)],
        compiler_params=params,
    )(me, mine, theirs, panel)
    return basis, factor


def solution(mesh):
    return jax.shard_map(
        on_device,
        mesh=mesh,
        in_specs=(
            P(("row", "col"), None),
            P("row", "col", None, None, None),
            P("row", "col", None),
            P("row", "col", None),
            P("row", "col"),
        ),
        out_specs=(P(("row", "col"), None), P()),
        check_vma=False,
    )
```
